32 devices in a mesh: dp: 2 (over core), cuts: 4 (over y, x), topic: 4 (over z).
Axes of the slice: x: 2, y: 2, z: 4, core: 2. Of those that a mesh axis runs over, the one named last changes fastest.
Arguments:
- doc_mix: float32 [2048, 4096], P(('dp', 'cuts'), 'topic'), may hold values from 0.01 to 1
- doc_lengths: int32 [2048], P(('dp', 'cuts')), may hold values from 1 to 4096, 524288 in all
- counts: int32 [2048, 256], P(('dp', 'cuts')), may hold values from 0 to 7
- tile_on: int32 [8, 4], P(('dp', 'cuts')), may hold values from 0 to 1, as said below
- word_counts: float32 [256, 4096], P('cuts', 'topic'), may hold values from 0.01 to 10
- topic_totals: float32 [4096], P('topic'), may hold values from 1000 to 100000
Outputs:
- doc_topic: float32 [2048, 4096], P(('dp', 'cuts'), 'topic')
- word_topic: float32 [256, 4096], P('cuts', 'topic')
The draws below stay inside these ranges and needn't reach their ends.
Inputs may be any that keep to these rules, and one draw needn't show every extreme that they name: `tile_on`: each block of documents meets at least one word slice.
All inputs are finite; a program needn't handle non-finite values. No bound on the sum of `doc_lengths` on one device may be relied on, other than what follows from the above.
Results may differ from the reference program's by a relative error of at most 0.000078.
Values sent between devices are 32-bit elements; how exact they have to be, the bound alone decides.
A program may use at most 64 MiB of HBM per device.

```python
import math
import jax
import jax.numpy as jnp
import numpy as np
from jax import lax

K = 4096
VOCAB = 1048576
WS = 64
DOC_DEV = 256
SLAB = 256
DOC_BLOCKS = 8
DOCS = 2048
N_CUTS = 4


def draw_tile_on(key, part):
    level_key = jax.random.fold_in(key, 11)
    cell_key = jax.random.fold_in(key, 12)
    levels = jax.random.randint(level_key, (DOC_BLOCKS, 1), 2, 9)
    cells = jax.random.randint(cell_key, (DOC_BLOCKS, N_CUTS), 0, 8)
    rows = jnp.arange(DOC_BLOCKS, dtype=jnp.int32)[:, None]
    cols = jnp.arange(N_CUTS, dtype=jnp.int32)[None, :]
    forced = cols == rows % N_CUTS
    return jnp.where((cells < levels) | forced, 1, 0).astype(jnp.int32)


def place_ends(entries, stream_key, smallest, largest):
    longest = entries.shape.index(max(entries.shape))
    spots = []
    for shift in (0, 1):
        where = [jax.random.randint(jax.random.fold_in(stream_key, axis), (), 0, length) for axis, length in enumerate(entries.shape)]
        where[longest] = (where[longest] + shift) % entries.shape[longest]
        spots.append(tuple(where))
    return entries.at[spots[0]].set(smallest).at[spots[1]].set(largest)


def block_levels(stream_key, shape, cuts, smallest, largest):
    factor_of = 1.0
    for axis_at, blocks in cuts:
        heights = jax.random.uniform(jax.random.fold_in(jax.random.fold_in(stream_key, 6), axis_at), (blocks,), jnp.float32, smallest / len(cuts), largest / len(cuts))
        factor_of = factor_of * jnp.repeat(jnp.exp(heights), shape[axis_at] // blocks).reshape((-1,) + (1,) * (len(shape) - 1 - axis_at))
    return factor_of


def length_profile(count, total, reach, slope):
    portions = [(1 << 20) // math.isqrt(grade ** slope) + 1 for grade in range(2, count + 1)]
    surplus, given = total - reach - (count - 1), [1] * (count - 1)
    while surplus > 0:
        free = [i for i in range(count - 1) if given[i] < reach]
        whole, budget = sum([portions[i] for i in free]), surplus
        for i in free:
            more = min(reach - given[i], max(1, budget * portions[i] // whole), surplus)
            given[i] = given[i] + more
            surplus = surplus - more
    return np.array([reach] + given)


def ragged_sizes(own_key, number_of, total, limit, skew):
    if number_of == 2:
        one = jax.random.randint(own_key, (), max(1, total - limit), min(limit, total - 1) + 1)
        return jnp.stack([one, total - one])
    tallies = jnp.asarray(length_profile(number_of, total, limit, skew), jnp.int32)
    couples = (number_of - 1) // 2
    donor, taker = tallies[1:1 + 2 * couples:2], tallies[2:2 + 2 * couples:2]
    slack = jnp.minimum(donor - 1, limit - taker)
    passed = jax.random.randint(jax.random.fold_in(own_key, 1), (couples,), 0, 1 << 20) % (slack + 1)
    tallies = tallies.at[1:1 + 2 * couples:2].set(donor - passed).at[2:2 + 2 * couples:2].set(taker + passed)
    return tallies[jax.random.permutation(jax.random.fold_in(own_key, 2), number_of)]


def setup_inputs(seed: int = 0) -> dict:
    keys = jax.random.split(jax.random.key(seed), 7)
    doc_mix = jnp.clip(jnp.exp(math.log(1.0) - 4.6051702 * jax.random.uniform(keys[0], (DOCS, K), jnp.float32) ** block_levels(keys[0], (DOCS, K), ((0, 8), (1, 4)), -0.2, 0.2)), 0.01, 1.0)
    doc_lengths = ragged_sizes(keys[1], DOCS, 256 * DOCS, 4096, 2).astype(jnp.int32)
    counts = place_ends(jax.random.randint(keys[2], (DOCS, SLAB), 0, 8), jax.random.fold_in(keys[2], 1), 0, 7).astype(jnp.int32)
    tile_on = draw_tile_on(jax.random.fold_in(keys[6], 71), 0)
    word_counts = jnp.clip(jnp.exp(math.log(10.0) - 6.9077553 * jax.random.uniform(keys[4], (SLAB, K), jnp.float32) ** block_levels(keys[4], (SLAB, K), ((0, 4), (1, 4)), -0.2, 0.2)), 0.01, 10.0)
    topic_totals = jnp.clip(jnp.exp(math.log(100000.0) - 4.6051702 * jax.random.uniform(keys[5], (K,), jnp.float32) ** block_levels(keys[5], (K,), ((0, 4),), -0.2, 0.2)), 1000.0, 100000.0)
    return dict(doc_mix=doc_mix, doc_lengths=doc_lengths, counts=counts, tile_on=tile_on, word_counts=word_counts, topic_totals=topic_totals)


ALPHA = 0.1
BETA = 0.01


def reference(doc_mix, doc_lengths, counts, tile_on, word_counts, topic_totals):
    mass = jnp.sum(doc_mix, axis=1, keepdims=True)
    doc_weight = doc_lengths.astype(jnp.float32)[:, None] * doc_mix / mass + ALPHA
    word_weight = (word_counts + BETA) / (topic_totals + VOCAB * BETA)[None, :]
    tile_mask = jnp.repeat(jnp.repeat(tile_on, DOC_DEV, axis=0), WS, axis=1)
    weights = (counts * tile_mask).astype(jnp.float32)
    denom = jnp.dot(doc_weight, word_weight.T, precision=lax.Precision.HIGHEST, preferred_element_type=jnp.float32)
    ratio = weights / denom
    doc_topic = doc_weight * jnp.dot(ratio, word_weight, precision=lax.Precision.HIGHEST, preferred_element_type=jnp.float32)
    word_topic = word_weight * jnp.dot(ratio.T, doc_weight, precision=lax.Precision.HIGHEST, preferred_element_type=jnp.float32)
    return doc_topic, word_topic
```

```python
import functools

import jax
import jax.numpy as jnp
from jax import lax
from jax.experimental import pallas as pl
from jax.experimental.pallas import tpu as pltpu
from jax.sharding import PartitionSpec as P

VOCAB = 1048576
ALPHA = 0.1
BETA = 0.01
F32, BF16 = jnp.float32, jnp.bfloat16
MESH = pl.DeviceIdType.MESH


def partner(index, step, size):
    total, bit = 0, 1
    while bit < size:
        a, b = (index // bit) % 2, (step // bit) % 2
        total = total + bit * (a + b - 2 * a * b)
        bit *= 2
    return total


def halves(x):
    hi = x.astype(BF16)
    return hi, (x - hi.astype(F32)).astype(BF16)


def mul(a, b, dims):
    return lax.dot_general(a, b, (dims, ((), ())), preferred_element_type=F32)


def mul3(a, b, dims):
    return mul(a[0], b[0], dims) + (mul(a[0], b[1], dims) + mul(a[1], b[0], dims))


def steps(first, last, body):
    if last - first <= 4:
        for step in range(first, last):
            body(step)
    else:
        lax.fori_loop(first, last, lambda i, z: (body(i), z)[1], 0)


def kernel(
    sizes, mix, lengths, counts, tile, wc, totals, doc_out, word_out,
    mass_send, mass_in, words, w_hi, w_lo, dw, d_hi, d_lo, counts_t,
    part, part_in, ratio, wsum, pair_in, reduced, cut_in,
    mass_s, mass_r, wg_s, wg_r, wf_s, wf_r, pt_s, pt_r, rt_s, rt_r,
    c1_s, c1_r, c2_s, c2_r, c4_s, c4_r,
):
    n_dp, n_cut, n_top = sizes
    ws, width = wc.shape
    docs = mix.shape[0]
    me_p, me_c, me_t = lax.axis_index("dp"), lax.axis_index("cuts"), lax.axis_index("topic")
    rows_p, rows_t = ws // n_dp, ws // n_top

    def dp(q):
        return {"dp": partner(me_p, q, n_dp)}

    def cut(r):
        return {"cuts": partner(me_c, r, n_cut)}

    def top(q):
        return {"topic": partner(me_t, q, n_top)}

    def sl(r):
        return partner(me_c, r, n_cut)

    def p_rows(s, p):
        return pl.ds(pl.multiple_of(s * ws + p * rows_p, rows_p), rows_p)

    def t_rows(s, t):
        return pl.ds(pl.multiple_of(s * ws + t * rows_t, rows_t), rows_t)

    def s_rows(s):
        return pl.ds(pl.multiple_of(s * ws, ws), ws)

    def rc(src, dst, ss, rs, dev):
        return pltpu.make_async_remote_copy(
            src_ref=src, dst_ref=dst, send_sem=ss, recv_sem=rs,
            device_id=dev, device_id_type=MESH)

    barrier = pltpu.get_barrier_semaphore()
    for size, dev in ((n_top, top), (n_cut, cut), (n_dp, dp)):
        for q in range(1, size):
            pl.semaphore_signal(barrier, inc=1, device_id=dev(q), device_id_type=MESH)

    words[s_rows(me_c), :] = (wc[...] + BETA) / (totals[...] + VOCAB * BETA)
    col = jnp.sum(mix[...], axis=1, keepdims=True)
    mass_send[...] = jnp.broadcast_to(col, (docs, 128)).T[0:8, :]
    pl.semaphore_wait(barrier, n_top + n_cut + n_dp - 3)

    def mass_copy(q, dst_step):
        return rc(mass_send, mass_in.at[dst_step], mass_s.at[q], mass_r.at[q], top(q))

    for q in range(1, n_top):
        mass_copy(q, q).start()

    def gather(r, s):
        rows = p_rows(s, me_p)
        return rc(words.at[rows, :], words.at[rows, :], wg_s.at[r], wg_r.at[r], cut(r))

    steps(1, n_cut, lambda r: gather(r, me_c).start())

    def forward(r, q, p):
        rows = p_rows(sl(r), p)
        return rc(words.at[rows, :], words.at[rows, :], wf_s.at[r, q], wf_r.at[r, q], dp(q))

    counts_t[...] = counts[...].astype(F32).T

    w_hi[s_rows(me_c), :], w_lo[s_rows(me_c), :] = halves(words[s_rows(me_c), :])

    mass = mass_send[...]
    for q in range(1, n_top):
        mass_copy(q, q).wait_recv()
        mass = mass + mass_in[q]
    scale = lengths[...].astype(F32) / mass[0:1, :]
    scale = jnp.broadcast_to(scale, (128, docs)).T[:, 0:1]
    weight = mix[...] * scale + ALPHA
    dw[...] = weight
    d_hi[...], d_lo[...] = halves(weight)

    def part_copy(r, q, s, t):
        return rc(part.at[t_rows(s, t), :], part_in.at[r, q], pt_s.at[r, q], pt_r.at[r, q], top(q))

    def denominators(r):
        s = sl(r)
        rows = s_rows(s)
        part[rows, :] = mul3((w_hi[rows, :], w_lo[rows, :]), (d_hi[...], d_lo[...]), ((1,), (1,)))
        for q in range(1, n_top):
            part_copy(r, q, s, partner(me_t, q, n_top)).start()

    def ratio_copy(r, q, t):
        rows = t_rows(sl(r), t)
        return rc(ratio.at[rows, :], ratio.at[rows, :], rt_s.at[r, q], rt_r.at[r, q], top(q))

    def ratios(r):
        s = sl(r)
        rows = t_rows(s, me_t)
        denom = part[rows, :]
        for q in range(1, n_top):
            part_copy(r, q, s, me_t).wait_recv()
            denom = denom + part_in[r, q]
        flag = tile[0, s].astype(F32)
        ratio[rows, :] = counts_t[rows, :] * flag / denom
        for q in range(1, n_top):
            ratio_copy(r, q, me_t).start()

    def pair_copy(r, q, p):
        return rc(wsum.at[p_rows(sl(r), p), :], pair_in.at[r, q], c1_s.at[r, q], c1_r.at[r, q], dp(q))

    def word_sums(r):
        rows = s_rows(sl(r))
        for q in range(1, n_top):
            ratio_copy(r, q, partner(me_t, q, n_top)).wait_recv()
        both = halves(ratio[rows, :])
        wsum[rows, :] = mul3(both, (d_hi[...], d_lo[...]), ((1,), (0,)))
        for q in range(1, n_dp):
            pair_copy(r, q, partner(me_p, q, n_dp)).start()

    def cut_copy(r):
        return rc(reduced.at[r], cut_in.at[r], c2_s.at[r], c2_r.at[r], cut(r))

    def reduce_pair(r):
        total = wsum[p_rows(sl(r), me_p), :]
        for q in range(1, n_dp):
            pair_copy(r, q, me_p).wait_recv()
            total = total + pair_in[r, q]
        reduced[r] = total

    def send_cut(r):
        reduce_pair(r)
        cut_copy(r).start()

    denominators(0)
    ratios(0)

    def pass_on(r):
        gather(r, sl(r)).wait_recv()
        for q in range(1, n_dp):
            forward(r, q, me_p).start()

    steps(1, n_cut, pass_on)

    def take(r):
        for q in range(1, n_dp):
            forward(r, q, partner(me_p, q, n_dp)).wait_recv()
        rows = s_rows(sl(r))
        w_hi[rows, :], w_lo[rows, :] = halves(words[rows, :])
        denominators(r)

    steps(1, n_cut, take)
    word_sums(0)
    steps(1, n_cut, ratios)

    def words_then_pair(r):
        word_sums(r)

    steps(1, n_cut, words_then_pair)
    steps(1, n_cut, send_cut)
    reduce_pair(0)

    left = halves(ratio[...].T)
    chunk = min(width, 256)
    for at in range(0, width, chunk):
        cols = slice(at, at + chunk)
        sums = mul3(left, (w_hi[:, cols], w_lo[:, cols]), ((1,), (0,)))
        doc_out[:, cols] = dw[:, cols] * sums

    def add_cut(r):
        cut_copy(r).wait_recv()
        reduced[0] = reduced[0] + cut_in[r]

    steps(1, n_cut, add_cut)
    mine = pl.ds(pl.multiple_of(me_p * rows_p, rows_p), rows_p)
    word_out[mine, :] = words[p_rows(me_c, me_p), :] * reduced[0]

    def last_copy(q, p):
        rows = pl.ds(pl.multiple_of(p * rows_p, rows_p), rows_p)
        return rc(word_out.at[rows, :], word_out.at[rows, :], c4_s.at[q], c4_r.at[q], dp(q))

    for q in range(1, n_dp):
        last_copy(q, me_p).start()

    for q in range(1, n_top):
        mass_copy(q, q).wait_send()

    def settle(r):
        for q in range(1, n_top):
            part_copy(r, q, sl(r), partner(me_t, q, n_top)).wait_send()
            ratio_copy(r, q, me_t).wait_send()
        for q in range(1, n_dp):
            pair_copy(r, q, partner(me_p, q, n_dp)).wait_send()

    def settle_cut(r):
        gather(r, me_c).wait_send()
        cut_copy(r).wait_send()
        for q in range(1, n_dp):
            forward(r, q, me_p).wait_send()

    steps(0, n_cut, settle)
    steps(1, n_cut, settle_cut)
    for q in range(1, n_dp):
        last_copy(q, me_p).wait_send()
        last_copy(q, partner(me_p, q, n_dp)).wait_recv()


def shards(sizes, doc_mix, doc_lengths, counts, tile_on, word_counts, topic_totals):
    n_dp, n_cut, n_top = sizes
    docs, width = doc_mix.shape
    ws = word_counts.shape[0]
    words = counts.shape[1]
    dma = pltpu.SemaphoreType.DMA
    vm = pltpu.VMEM
    vspec = pl.BlockSpec(memory_space=pltpu.VMEM)
    return pl.pallas_call(
        functools.partial(kernel, sizes),
        out_shape=(
            jax.ShapeDtypeStruct((docs, width), F32),
            jax.ShapeDtypeStruct((ws, width), F32),
        ),
        in_specs=[vspec, vspec, vspec, pl.BlockSpec(memory_space=pltpu.SMEM), vspec, vspec],
        out_specs=(vspec, vspec),
        scratch_shapes=[
            vm((8, docs), F32),
            vm((n_top, 8, docs), F32),
            vm((words, width), F32),
            vm((words, width), BF16),
            vm((words, width), BF16),
            vm((docs, width), F32),
            vm((docs, width), BF16),
            vm((docs, width), BF16),
            vm((words, docs), F32),
            vm((words, docs), F32),
            vm((n_cut, n_top, ws // n_top, docs), F32),
            vm((words, docs), F32),
            vm((words, width), F32),
            vm((n_cut, n_dp, ws // n_dp, width), F32),
            vm((n_cut, ws // n_dp, width), F32),
            vm((n_cut, ws // n_dp, width), F32),
            dma((n_top,)), dma((n_top,)),
            dma((n_cut,)), dma((n_cut,)),
            dma((n_cut, n_dp)), dma((n_cut, n_dp)),
            dma((n_cut, n_top)), dma((n_cut, n_top)),
            dma((n_cut, n_top)), dma((n_cut, n_top)),
            dma((n_cut, n_dp)), dma((n_cut, n_dp)),
            dma((n_cut,)), dma((n_cut,)),
            dma((n_dp,)), dma((n_dp,)),
        ],
        compiler_params=pltpu.CompilerParams(
            collective_id=0, has_side_effects=True, vmem_limit_bytes=44 * 1024 * 1024),
        cost_estimate=pl.CostEstimate(
            flops=6 * docs * words * width, transcendentals=0,
            bytes_accessed=4 * (2 * docs * width + docs * words + 2 * ws * width)),
    )(doc_mix, doc_lengths[None, :], counts, tile_on, word_counts, topic_totals[None, :])


def solution(mesh):
    sizes = (mesh.shape["dp"], mesh.shape["cuts"], mesh.shape["topic"])
    return jax.shard_map(
        functools.partial(shards, sizes),
        mesh=mesh,
        in_specs=(
            P(("dp", "cuts"), "topic"),
            P(("dp", "cuts")),
            P(("dp", "cuts"), None),
            P(("dp", "cuts"), None),
            P("cuts", "topic"),
            P("topic"),
        ),
        out_specs=(P(("dp", "cuts"), "topic"), P("cuts", "topic")),
        check_vma=False,
    )
```

```python
import functools

import jax
import jax.numpy as jnp
from jax import lax
from jax.experimental import pallas as pl
from jax.experimental.pallas import tpu as pltpu
from jax.sharding import PartitionSpec as P

VOCAB = 1048576
ALPHA = 0.1
BETA = 0.01
F32, BF16 = jnp.float32, jnp.bfloat16
MESH = pl.DeviceIdType.MESH


def partner(index, step, size):
    total, bit = 0, 1
    while bit < size:
        a, b = (index // bit) % 2, (step // bit) % 2
        total = total + bit * (a + b - 2 * a * b)
        bit *= 2
    return total


def halves(x):
    hi = x.astype(BF16)
    return hi, (x - hi.astype(F32)).astype(BF16)


def mul(a, b, dims):
    return lax.dot_general(a, b, (dims, ((), ())), preferred_element_type=F32)


def mul3(a, b, dims):
    return mul(a[0], b[0], dims) + (mul(a[0], b[1], dims) + mul(a[1], b[0], dims))


def steps(first, last, body):
    if last - first <= 4:
        for step in range(first, last):
            body(step)
    else:
        lax.fori_loop(first, last, lambda i, z: (body(i), z)[1], 0)


def kernel(
    sizes, mix_h, lengths_h, counts_h, tile_h, wc_h, totals_h, doc_out, word_out,
    mix, lengths, counts, tile, wc, totals, in_s,
    mass_send, mass_in, words, w_hi, w_lo, dw, d_hi, d_lo, counts_t,
    part, part_in, ratio, wsum, pair_in, reduced, cut_in,
    mass_s, mass_r, wg_s, wg_r, wf_s, wf_r, pt_s, pt_r, rt_s, rt_r,
    c1_s, c1_r, c2_s, c2_r, c4_s, c4_r,
):
    n_dp, n_cut, n_top = sizes
    ws, width = wc.shape
    docs = mix.shape[0]
    me_p, me_c, me_t = lax.axis_index("dp"), lax.axis_index("cuts"), lax.axis_index("topic")
    rows_p, rows_t = ws // n_dp, ws // n_top

    def dp(q):
        return {"dp": partner(me_p, q, n_dp)}

    def cut(r):
        return {"cuts": partner(me_c, r, n_cut)}

    def top(q):
        return {"topic": partner(me_t, q, n_top)}

    def sl(r):
        return partner(me_c, r, n_cut)

    def p_rows(s, p):
        return pl.ds(pl.multiple_of(s * ws + p * rows_p, rows_p), rows_p)

    def t_rows(s, t):
        return pl.ds(pl.multiple_of(s * ws + t * rows_t, rows_t), rows_t)

    def s_rows(s):
        return pl.ds(pl.multiple_of(s * ws, ws), ws)

    def rc(src, dst, ss, rs, dev):
        return pltpu.make_async_remote_copy(
            src_ref=src, dst_ref=dst, send_sem=ss, recv_sem=rs,
            device_id=dev, device_id_type=MESH)

    barrier = pltpu.get_barrier_semaphore()
    for size, dev in ((n_top, top), (n_cut, cut), (n_dp, dp)):
        for q in range(1, size):
            pl.semaphore_signal(barrier, inc=1, device_id=dev(q), device_id_type=MESH)

    loads = [
        pltpu.make_async_copy(src, dst, in_s.at[i])
        for i, (src, dst) in enumerate((
            (totals_h, totals), (wc_h, wc), (mix_h, mix),
            (lengths_h, lengths), (tile_h, tile), (counts_h, counts)))
    ]
    for load in loads:
        load.start()
    loads[0].wait()
    loads[1].wait()
    words[s_rows(me_c), :] = (wc[...] + BETA) / (totals[...] + VOCAB * BETA)
    pl.semaphore_wait(barrier, n_top + n_cut + n_dp - 3)

    def mass_copy(q, dst_step):
        return rc(mass_send, mass_in.at[dst_step], mass_s.at[q], mass_r.at[q], top(q))

    def gather(r, s):
        rows = p_rows(s, me_p)
        return rc(words.at[rows, :], words.at[rows, :], wg_s.at[r], wg_r.at[r], cut(r))

    steps(1, n_cut, lambda r: gather(r, me_c).start())

    loads[2].wait()
    col = jnp.sum(mix[...], axis=1, keepdims=True)
    mass_send[...] = jnp.broadcast_to(col, (docs, 128)).T[0:8, :]
    for q in range(1, n_top):
        mass_copy(q, q).start()

    def forward(r, q, p):
        rows = p_rows(sl(r), p)
        return rc(words.at[rows, :], words.at[rows, :], wf_s.at[r, q], wf_r.at[r, q], dp(q))

    for load in loads[3:]:
        load.wait()
    counts_t[...] = counts[...].astype(F32).T

    w_hi[s_rows(me_c), :], w_lo[s_rows(me_c), :] = halves(words[s_rows(me_c), :])

    mass = mass_send[...]
    for q in range(1, n_top):
        mass_copy(q, q).wait_recv()
        mass = mass + mass_in[q]
    scale = lengths[...].astype(F32) / mass[0:1, :]
    scale = jnp.broadcast_to(scale, (128, docs)).T[:, 0:1]
    weight = mix[...] * scale + ALPHA
    dw[...] = weight
    d_hi[...], d_lo[...] = halves(weight)

    def part_copy(r, q, s, t):
        return rc(part.at[t_rows(s, t), :], part_in.at[r, q], pt_s.at[r, q], pt_r.at[r, q], top(q))

    def denominators(r):
        s = sl(r)
        rows = s_rows(s)
        part[rows, :] = mul3((w_hi[rows, :], w_lo[rows, :]), (d_hi[...], d_lo[...]), ((1,), (1,)))
        for q in range(1, n_top):
            part_copy(r, q, s, partner(me_t, q, n_top)).start()

    def ratio_copy(r, q, t):
        rows = t_rows(sl(r), t)
        return rc(ratio.at[rows, :], ratio.at[rows, :], rt_s.at[r, q], rt_r.at[r, q], top(q))

    def ratios(r):
        s = sl(r)
        rows = t_rows(s, me_t)
        denom = part[rows, :]
        for q in range(1, n_top):
            part_copy(r, q, s, me_t).wait_recv()
            denom = denom + part_in[r, q]
        place = lax.broadcasted_iota(jnp.int32, (1, n_cut), 1)
        flag = jnp.sum(jnp.where(place == s, tile[...], 0).astype(F32), axis=1, keepdims=True)
        ratio[rows, :] = counts_t[rows, :] * flag / denom
        for q in range(1, n_top):
            ratio_copy(r, q, me_t).start()

    def pair_copy(r, q, p):
        return rc(wsum.at[p_rows(sl(r), p), :], pair_in.at[r, q], c1_s.at[r, q], c1_r.at[r, q], dp(q))

    def word_sums(r):
        rows = s_rows(sl(r))
        for q in range(1, n_top):
            ratio_copy(r, q, partner(me_t, q, n_top)).wait_recv()
        both = halves(ratio[rows, :])
        wsum[rows, :] = mul3(both, (d_hi[...], d_lo[...]), ((1,), (0,)))
        for q in range(1, n_dp):
            pair_copy(r, q, partner(me_p, q, n_dp)).start()

    def cut_copy(r):
        return rc(reduced.at[r], cut_in.at[r], c2_s.at[r], c2_r.at[r], cut(r))

    def reduce_pair(r):
        total = wsum[p_rows(sl(r), me_p), :]
        for q in range(1, n_dp):
            pair_copy(r, q, me_p).wait_recv()
            total = total + pair_in[r, q]
        reduced[r] = total

    def send_cut(r):
        reduce_pair(r)
        cut_copy(r).start()

    def pass_on(r):
        gather(r, sl(r)).wait_recv()
        for q in range(1, n_dp):
            forward(r, q, me_p).start()

    def take(r):
        for q in range(1, n_dp):
            forward(r, q, partner(me_p, q, n_dp)).wait_recv()
        rows = s_rows(sl(r))
        w_hi[rows, :], w_lo[rows, :] = halves(words[rows, :])
        denominators(r)

    denominators(0)
    if n_cut == 4:
        pass_on(1)
        pass_on(2)
        ratios(0)
        take(1)
        take(2)
        pass_on(3)
        ratios(1)
        take(3)
        word_sums(0)
        ratios(2)
        word_sums(1)
        ratios(3)
        send_cut(1)
        word_sums(2)
        send_cut(2)
        word_sums(3)
        send_cut(3)
    else:
        ratios(0)
        steps(1, n_cut, pass_on)
        steps(1, n_cut, take)
        word_sums(0)
        steps(1, n_cut, ratios)
        steps(1, n_cut, word_sums)
        steps(1, n_cut, send_cut)
    reduce_pair(0)

    left = halves(ratio[...].T)
    chunk = min(width, 256)
    for at in range(0, width, chunk):
        cols = slice(at, at + chunk)
        sums = mul3(left, (w_hi[:, cols], w_lo[:, cols]), ((1,), (0,)))
        doc_out[:, cols] = dw[:, cols] * sums

    def add_cut(r):
        cut_copy(r).wait_recv()
        reduced[0] = reduced[0] + cut_in[r]

    steps(1, n_cut, add_cut)
    mine = pl.ds(pl.multiple_of(me_p * rows_p, rows_p), rows_p)
    word_out[mine, :] = words[p_rows(me_c, me_p), :] * reduced[0]

    def last_copy(q, p):
        rows = pl.ds(pl.multiple_of(p * rows_p, rows_p), rows_p)
        return rc(word_out.at[rows, :], word_out.at[rows, :], c4_s.at[q], c4_r.at[q], dp(q))

    for q in range(1, n_dp):
        last_copy(q, me_p).start()

    for q in range(1, n_top):
        mass_copy(q, q).wait_send()

    def settle(r):
        for q in range(1, n_top):
            part_copy(r, q, sl(r), partner(me_t, q, n_top)).wait_send()
            ratio_copy(r, q, me_t).wait_send()
        for q in range(1, n_dp):
            pair_copy(r, q, partner(me_p, q, n_dp)).wait_send()

    def settle_cut(r):
        gather(r, me_c).wait_send()
        cut_copy(r).wait_send()
        for q in range(1, n_dp):
            forward(r, q, me_p).wait_send()

    steps(0, n_cut, settle)
    steps(1, n_cut, settle_cut)
    for q in range(1, n_dp):
        last_copy(q, me_p).wait_send()
        last_copy(q, partner(me_p, q, n_dp)).wait_recv()


def shards(sizes, doc_mix, doc_lengths, counts, tile_on, word_counts, topic_totals):
    n_dp, n_cut, n_top = sizes
    docs, width = doc_mix.shape
    ws = word_counts.shape[0]
    words = counts.shape[1]
    dma = pltpu.SemaphoreType.DMA
    vm = pltpu.VMEM
    vspec = pl.BlockSpec(memory_space=pltpu.VMEM)
    return pl.pallas_call(
        functools.partial(kernel, sizes),
        out_shape=(
            jax.ShapeDtypeStruct((docs, width), F32),
            jax.ShapeDtypeStruct((ws, width), F32),
        ),
        in_specs=[pl.BlockSpec(memory_space=pltpu.HBM)] * 6,
        out_specs=(vspec, vspec),
        scratch_shapes=[
            vm((docs, width), F32),
            vm((1, docs), jnp.int32),
            vm((docs, words), jnp.int32),
            vm((1, n_cut), jnp.int32),
            vm((ws, width), F32),
            vm((1, width), F32),
            dma((6,)),
            vm((8, docs), F32),
            vm((n_top, 8, docs), F32),
            vm((words, width), F32),
            vm((words, width), BF16),
            vm((words, width), BF16),
            vm((docs, width), F32),
            vm((docs, width), BF16),
            vm((docs, width), BF16),
            vm((words, docs), F32),
            vm((words, docs), F32),
            vm((n_cut, n_top, ws // n_top, docs), F32),
            vm((words, docs), F32),
            vm((words, width), F32),
            vm((n_cut, n_dp, ws // n_dp, width), F32),
            vm((n_cut, ws // n_dp, width), F32),
            vm((n_cut, ws // n_dp, width), F32),
            dma((n_top,)), dma((n_top,)),
            dma((n_cut,)), dma((n_cut,)),
            dma((n_cut, n_dp)), dma((n_cut, n_dp)),
            dma((n_cut, n_top)), dma((n_cut, n_top)),
            dma((n_cut, n_top)), dma((n_cut, n_top)),
            dma((n_cut, n_dp)), dma((n_cut, n_dp)),
            dma((n_cut,)), dma((n_cut,)),
            dma((n_dp,)), dma((n_dp,)),
        ],
        compiler_params=pltpu.CompilerParams(
            collective_id=0, has_side_effects=True, vmem_limit_bytes=62 * 1024 * 1024),
        cost_estimate=pl.CostEstimate(
            flops=6 * docs * words * width, transcendentals=0,
            bytes_accessed=4 * (2 * docs * width + docs * words + 2 * ws * width)),
    )(doc_mix, doc_lengths[None, :], counts, tile_on, word_counts, topic_totals[None, :])


def solution(mesh):
    sizes = (mesh.shape["dp"], mesh.shape["cuts"], mesh.shape["topic"])
    return jax.shard_map(
        functools.partial(shards, sizes),
        mesh=mesh,
        in_specs=(
            P(("dp", "cuts"), "topic"),
            P(("dp", "cuts")),
            P(("dp", "cuts"), None),
            P(("dp", "cuts"), None),
            P("cuts", "topic"),
            P("topic"),
        ),
        out_specs=(P(("dp", "cuts"), "topic"), P("cuts", "topic")),
        check_vma=False,
    )
```
